32 devices in a mesh: tgt: 8 (over z, x), src: 4 (over y, core).
Axes of the slice: x: 2, y: 2, z: 4, core: 2. Of those that a mesh axis runs over, the one named last changes fastest.
Arguments:
- points: bfloat16 [65536, 256], P(('tgt', 'src')), may hold values from -0.4 to 0.4
- weights: bfloat16 [65536, 64], P(('tgt', 'src')), may hold values from -6 to 6
- near_list: int32 [512, 16], P(('tgt', 'src')), may hold values from -1 to 63, as said below
- far_list: int32 [512, 3, 4], P('tgt', None, 'src'), may hold values from -1 to 31, as said below
- skel_index: int32 [224, 256], P(('tgt', 'src')), may hold values from 0 to 2047, as said below
- equiv_weights: bfloat16 [224, 256, 64], P(('tgt', 'src')), may hold values from -6 to 6
Outputs:
- potential: float32 [65536, 64], P(('tgt', 'src'))
The draws below stay inside these ranges and needn't reach their ends.
Inputs may be any that keep to these rules, and one draw needn't show every extreme that they name: `near_list`: row b lists blocks of b's group of 64 blocks by their index within the group: first b itself, then distinct other blocks; after a row's live entries all are -1; every row has 4 or more live entries. `far_list`: entry [b, l, c] is -1 or a level-l node owned by a device of src index c, numbered as the owner's tgt index times (16 // (4 * 2 ** l)) plus the node's number among the owner's level-l nodes. `skel_index`: Level-l nodes of a device cover 4 * 128 * 2 ** l consecutive points of that device each, in order; a node's 256 entries are increasing indices of the device's points inside the node.
All inputs are finite; a program needn't handle non-finite values.
Results may differ from the reference program's by a relative error of at most 0.0023.
Values may be sent and summed in bfloat16 or wider, within the bound.
A program may use at most 192 MiB of HBM per device.

```python
import jax
import jax.numpy as jnp
from jax import lax

E = 256
WCOL = 64
BLK = 128
RANK = 256
NEAR = 16
LEVELS = 3
BLK_DEV = 16
NODE_DEV = 7
NPTS = 65536
NODES = 224
N_TGT = 8
N_SRC = 4
DEVICES = 32


def random_signs(key, shape):
    return 2.0 * jax.random.randint(key, shape, 0, 2).astype(jnp.float32) - 1.0


def draw_points(key, part):
    centre_size = 0.09
    scale_low = 0.85
    scale_high = 1.15
    noise = jnp.clip(0.0625 * jax.random.normal(jax.random.fold_in(key, 44), (DEVICES, BLK_DEV, BLK, E), jnp.float32), -0.25, 0.25)
    centre = centre_size * random_signs(jax.random.fold_in(key, 41), (E,))
    device_part = 0.02 * random_signs(jax.random.fold_in(key, 42), (DEVICES, E))
    block_scale = jax.random.uniform(jax.random.fold_in(key, 43), (DEVICES, BLK_DEV, 1, 1), jnp.float32, scale_low, scale_high)
    base = (centre[None, :] + device_part)[:, None, None, :]
    values = block_scale * base + noise
    return values.reshape(DEVICES * BLK_DEV * BLK, E).astype(jnp.bfloat16)


def draw_near_list(key, part):
    group_blocks = N_SRC * BLK_DEV
    row_count = BLK_DEV * DEVICES
    row_ids = jnp.arange(row_count, dtype=jnp.int32)
    own_block = row_ids % group_blocks
    row_keys = jax.random.split(jax.random.fold_in(key, 11), row_count)

    def pick_neighbours(row_key):
        return jax.random.permutation(row_key, group_blocks - 1)[:NEAR - 1]
    neighbours = jax.vmap(pick_neighbours)(row_keys).astype(jnp.int32)
    neighbours = (own_block[:, None] + 1 + neighbours) % group_blocks
    entries = jnp.concatenate([own_block[:, None], neighbours], axis=1)
    device_shift = jax.random.randint(jax.random.fold_in(key, 12), (DEVICES,), 0, 3)
    device_cap = jnp.right_shift(jnp.int32(NEAR), device_shift)[row_ids // BLK_DEV]
    live_count = jax.random.randint(jax.random.fold_in(key, 13), (row_count,), NEAR // 4, NEAR + 1)
    live_count = jnp.minimum(live_count, jnp.maximum(device_cap, NEAR // 4))
    live_count = live_count.at[0].set(NEAR).at[1].set(NEAR // 4)
    slot_index = jnp.arange(NEAR, dtype=jnp.int32)[None, :]
    return jnp.where(slot_index < live_count[:, None], entries, -1).astype(jnp.int32)


def draw_far_list(key, part):
    row_count = BLK_DEV * DEVICES
    level_sizes = jnp.array([N_TGT * (BLK_DEV // (4 * 2 ** tree_level)) for tree_level in range(LEVELS)], jnp.int32)
    raw_draw = jax.random.randint(jax.random.fold_in(key, 21), (row_count, LEVELS, N_SRC), 0, 16777216)
    values = raw_draw % level_sizes[None, :, None]
    is_live = jax.random.randint(jax.random.fold_in(key, 22), (row_count, LEVELS, N_SRC), 0, 4) < 3
    values = values.at[0, 0, :].set(level_sizes[0] - 1)
    is_live = is_live.at[0].set(True).at[1].set(False)
    return jnp.where(is_live, values, -1).astype(jnp.int32)


def draw_skel_index(key, part):
    row_count = NODE_DEV * DEVICES
    local_node = jnp.arange(row_count, dtype=jnp.int32) % NODE_DEV
    first_count = BLK_DEV // 4
    second_count = BLK_DEV // 8
    tree_level = (local_node >= first_count).astype(jnp.int32) + (local_node >= first_count + second_count).astype(jnp.int32)
    within = local_node - jnp.where(tree_level == 0, 0, jnp.where(tree_level == 1, first_count, first_count + second_count))
    node_size = jnp.left_shift(jnp.int32(4 * BLK), tree_level)
    stride_size = node_size // RANK
    jitter = jax.random.randint(jax.random.fold_in(key, 31), (row_count, RANK), 0, 16777216) % stride_size[:, None]
    jitter = jitter.at[:, 0].set(0)
    jitter = jitter.at[:, RANK - 1].set(stride_size - 1)
    offset = jnp.arange(RANK, dtype=jnp.int32)[None, :] * stride_size[:, None] + jitter
    return ((within * node_size)[:, None] + offset).astype(jnp.int32)


def shard_levels(own_key, shape, pieces, least, top_value):
    def one(dim, parts):
        heights = jax.random.uniform(jax.random.fold_in(jax.random.fold_in(own_key, 6), dim), (parts,), jnp.float32, least / len(pieces), top_value / len(pieces))
        return jnp.repeat(jnp.exp(heights), shape[dim] // parts).reshape((-1,) + (1,) * (len(shape) - dim - 1))

    factor_of = one(*pieces[0])
    for cut in pieces[1:]:
        factor_of = factor_of * one(*cut)
    return factor_of


def bell_draw(own_key, shape, deviation, reach, cuts=(), held_as=jnp.bfloat16):
    gain = shard_levels(own_key, shape, cuts, -0.22, 0.18) if cuts else 1.0
    values = jax.random.normal(own_key, shape, jnp.float32) * deviation * gain
    return jnp.minimum(jnp.maximum(values, -reach), reach).astype(held_as)


def setup_inputs(seed: int = 0) -> dict:
    arg_keys = jax.random.split(jax.random.key(seed), 7)
    points = draw_points(jax.random.fold_in(arg_keys[6], 71), 0)
    weights = bell_draw(arg_keys[1], (NPTS, WCOL), 1.0, 6.0, ((0, 32),))
    near_list = draw_near_list(jax.random.fold_in(arg_keys[6], 71), 0)
    far_list = draw_far_list(jax.random.fold_in(arg_keys[6], 71), 0)
    skel_index = draw_skel_index(jax.random.fold_in(arg_keys[6], 71), 0)
    equiv_weights = bell_draw(arg_keys[5], (NODES, RANK, WCOL), 1.0, 6.0, ((0, 32),))
    return {"points": points, "weights": weights, "near_list": near_list, "far_list": far_list, "skel_index": skel_index, "equiv_weights": equiv_weights}


kernel_rate = 2.0


def tile_kernel(targets, target_norms, sources, source_norms, live_mask):
    dot_terms = jnp.einsum("bie,bse->bis", targets.astype(jnp.float32), sources.astype(jnp.float32))
    sq_dist = target_norms[:, :, None] + source_norms[:, None, :] - 2.0 * dot_terms
    return jnp.where(live_mask[:, None, :], jnp.exp(-kernel_rate * sq_dist), 0.0).astype(jnp.bfloat16)


def apply_tile(kernel, source_weights):
    return jnp.einsum("bis,bsw->biw", kernel.astype(jnp.float32), source_weights.astype(jnp.float32))


def reference(points, weights, near_list, far_list, skel_index, equiv_weights):
    point_dev = BLK_DEV * BLK
    group_blocks = N_SRC * BLK_DEV
    group_points = N_SRC * point_dev
    node_dev = skel_index.shape[0] // (N_TGT * N_SRC)
    point_norms = jnp.sum(jnp.square(points.astype(jnp.float32)), axis=1)
    level_nodes = [BLK_DEV // (4 * 2 ** tree_level) for tree_level in range(LEVELS)]
    level_start = [sum(level_nodes[:tree_level]) for tree_level in range(LEVELS)]
    columns = jnp.arange(N_SRC, dtype=jnp.int32)

    def one_group(group_index):
        row_base = group_index * group_points
        group_pts = lax.dynamic_slice_in_dim(points, row_base, group_points, 0).reshape(group_blocks, BLK, E)
        group_norms = lax.dynamic_slice_in_dim(point_norms, row_base, group_points, 0).reshape(group_blocks, BLK)
        group_wts = lax.dynamic_slice_in_dim(weights, row_base, group_points, 0).reshape(group_blocks, BLK, WCOL)
        near_rows = lax.dynamic_slice_in_dim(near_list, group_index * group_blocks, group_blocks, 0)
        near_live = near_rows >= 0
        near_index = jnp.where(near_live, near_rows, 0)
        near_src = group_pts[near_index].reshape(group_blocks, NEAR * BLK, E)
        near_norm = group_norms[near_index].reshape(group_blocks, NEAR * BLK)
        near_wts = group_wts[near_index].reshape(group_blocks, NEAR * BLK, WCOL)
        near_mask = jnp.repeat(near_live, BLK, axis=1)
        potential = apply_tile(tile_kernel(group_pts, group_norms, near_src, near_norm, near_mask), near_wts)
        far_rows = lax.dynamic_slice_in_dim(far_list, group_index * group_blocks, group_blocks, 0)
        for tree_level in range(LEVELS):
            far_entry = far_rows[:, tree_level, :]
            far_live = far_entry >= 0
            far_entry = jnp.where(far_live, far_entry, 0)
            owner_device = (far_entry // level_nodes[tree_level]) * N_SRC + columns[None, :]
            node_rows = owner_device * node_dev + level_start[tree_level] + far_entry % level_nodes[tree_level]
            point_rows = owner_device[:, :, None] * point_dev + skel_index[node_rows]
            skel_pts = points[point_rows].reshape(group_blocks, N_SRC * RANK, E)
            skel_norms = point_norms[point_rows].reshape(group_blocks, N_SRC * RANK)
            skel_wts = equiv_weights[node_rows].reshape(group_blocks, N_SRC * RANK, WCOL)
            far_mask = jnp.repeat(far_live, RANK, axis=1)
            potential = potential + apply_tile(tile_kernel(group_pts, group_norms, skel_pts, skel_norms, far_mask), skel_wts)
        return potential.reshape(group_points, WCOL)

    result = lax.map(one_group, jnp.arange(N_TGT, dtype=jnp.int32))
    return result.reshape(N_TGT * group_points, WCOL)
```

```python
import functools

import jax
import jax.numpy as jnp
from jax import lax
from jax.experimental import pallas as pl
from jax.experimental.pallas import tpu as pltpu
from jax.sharding import PartitionSpec as P

E = 256
WCOL = 64
BLK = 128
RANK = 256
NEAR = 16
LEVELS = 3
Z = 4

BROWS = BLK + BLK // 4
NROWS = RANK + RANK // 4
MESH = pl.DeviceIdType.MESH


def pack(w):
    q = w.shape[0] // 4
    return jnp.concatenate([w[k * q : (k + 1) * q, :] for k in range(4)], axis=1)


def unpack(p):
    return jnp.concatenate([p[:, k * WCOL : (k + 1) * WCOL] for k in range(4)], axis=0)


def row_norms(x):
    sq = jnp.square(x.astype(jnp.float32))
    hi = sq.astype(jnp.bfloat16)
    lo = (sq - hi.astype(jnp.float32)).astype(jnp.bfloat16)
    twos = jnp.full((16, E), 2.0, jnp.bfloat16)
    dims = (((1,), (1,)), ((), ()))
    total = lax.dot_general(twos, hi, dims, preferred_element_type=jnp.float32)
    total = total + lax.dot_general(twos, lo, dims, preferred_element_type=jnp.float32)
    return total[0:1, :]


def targets_of(x):
    sq = jnp.square(x.astype(jnp.float32))
    return x * jnp.bfloat16(4.0), 2.0 * jnp.sum(sq, axis=1, keepdims=True)


def tile(xt, tn, src, sn, w):
    d = lax.dot_general(xt, src, (((1,), (1,)), ((), ())), preferred_element_type=jnp.float32)
    k = jnp.exp((d - tn) - sn).astype(jnp.bfloat16)
    return jnp.dot(k, w, preferred_element_type=jnp.float32)


def kernel(
    n_tgt, n_src, blk_dev, level_nodes,
    pts, wts, skel, ew, near, far, out,
    grp, gn, l0, l1, l2, n0, n1, n2, facc, red_out, red_in,
    gs, gr, zs, zr, xs, xr, rs, rr,
):
    X = n_tgt // Z
    tgt, src = lax.axis_index("tgt"), lax.axis_index("src")
    z, x = tgt // X, tgt % X
    levels, norms = (l0, l1, l2), (n0, n1, n2)
    pairs = blk_dev // 2

    def z_peer(k):
        return lax.rem(z + k, Z) * X + x

    def x_peer(k):
        return z * X + lax.rem(x + k, X)

    def s_peer(k):
        return lax.rem(src + k, n_src)

    barrier = pltpu.get_barrier_semaphore()
    for k in range(1, Z):
        pl.semaphore_signal(barrier, inc=1, device_id=(z_peer(k), src), device_id_type=MESH)
    for k in range(1, X):
        pl.semaphore_signal(barrier, inc=1, device_id=(x_peer(k), src), device_id_type=MESH)
    for k in range(1, n_src):
        pl.semaphore_signal(barrier, inc=1, device_id=(tgt, s_peer(k)), device_id_type=MESH)

    def z_copy(l, k):
        own = levels[l].at[pl.ds(tgt * level_nodes[l], level_nodes[l])]
        return pltpu.make_async_remote_copy(
            own, own, zs.at[l * Z + k], zr.at[l * Z + k], (z_peer(k), src), MESH
        )

    def shard_of(k):
        return lax.rem(z - k + Z, Z) * X + x

    def x_copy(l, k, j):
        held = levels[l].at[pl.ds(shard_of(k) * level_nodes[l], level_nodes[l])]
        i = (l * Z + k) * X + j
        return pltpu.make_async_remote_copy(held, held, xs.at[i], xr.at[i], (x_peer(j), src), MESH)

    def g_copy(k):
        own = grp.at[pl.ds(src * blk_dev, blk_dev)]
        return pltpu.make_async_remote_copy(own, own, gs.at[k], gr.at[k], (tgt, s_peer(k)), MESH)

    def r_copy(k):
        return pltpu.make_async_remote_copy(
            red_out.at[k], red_in.at[k], rs.at[k], rr.at[k], (tgt, s_peer(k)), MESH
        )

    def gather_level(l):
        size = 4 * BLK * 2**l
        start = sum(level_nodes[:l])
        for r in range(level_nodes[l]):
            node = start + r
            acc = jnp.zeros((RANK, E), jnp.float32)
            for c in range(size // 512):
                base = r * size + c * 512
                pick = lax.broadcasted_iota(jnp.int32, (RANK, 512), 1) == skel[:, node : node + 1] - base
                pick = jnp.where(pick, 1.0, 0.0).astype(jnp.bfloat16)
                acc = acc + jnp.dot(pick, pts[base : base + 512, :], preferred_element_type=jnp.float32)
            at = tgt * level_nodes[l] + r
            levels[l][at, 0:RANK, :] = acc.astype(jnp.bfloat16)
            levels[l][at, RANK:NROWS, :] = pack(ew[node])

    def level_norms(l, shard):
        def body(r, c):
            at = shard * level_nodes[l] + r
            norms[l][at] = row_norms(levels[l][at, 0:RANK, :])
            return c
        lax.fori_loop(0, level_nodes[l], body, 0)

    gather_level(2)
    pl.semaphore_wait(barrier, (Z - 1) + (X - 1) + (n_src - 1))

    def send_level(l):
        for k in range(1, Z):
            z_copy(l, k).start()
        for j in range(1, X):
            x_copy(l, 0, j).start()

    send_level(2)
    gather_level(1)
    send_level(1)
    gather_level(0)
    send_level(0)

    def pack_block(b, c):
        at = src * blk_dev + b
        grp[at, 0:BLK, :] = pts[pl.ds(pl.multiple_of(b * BLK, BLK), BLK), :]
        grp[at, BLK:BROWS, :] = pack(wts[pl.ds(pl.multiple_of(b * BLK, BLK), BLK), :])
        return c

    lax.fori_loop(0, blk_dev, pack_block, 0)
    for k in range(1, n_src):
        g_copy(k).start()

    def forward(l, k):
        z_copy(l, k).wait_recv()
        for j in range(1, X):
            x_copy(l, k, j).start()

    def finish(l):
        for k in range(Z):
            for j in range(1, X):
                x_copy(l, k, j).wait_recv()
                level_norms(l, lax.rem(z - k + Z, Z) * X + lax.rem(x - j + X, X))

    for l in (2, 1, 0):
        level_norms(l, tgt)
    for l in (2, 1):
        for k in range(1, Z):
            forward(l, k)
            level_norms(l, shard_of(k))

    for k in range(1, n_src):
        g_copy(k).wait_recv()

    def group_norms(b, c):
        gn[b] = row_norms(grp[b, 0:BLK, :])
        return c

    lax.fori_loop(0, n_src * blk_dev, group_norms, 0)

    def far_block(l, b):
        xt, tn = targets_of(grp[b, 0:BLK, :])
        e = far[l, b]
        i = jnp.maximum(e, 0)
        sn = norms[l][i] + jnp.where(e >= 0, 0.0, 1e30)
        return tile(xt, tn, levels[l][i, 0:RANK, :], sn, unpack(levels[l][i, RANK:NROWS, :]))

    def far_pair(l, p):
        return jnp.concatenate([far_block(l, 2 * p), far_block(l, 2 * p + 1)], axis=1)

    def near_block(b, c):
        rows = pl.ds(pl.multiple_of(b * BLK, BLK), BLK)
        xt, tn = targets_of(pts[rows, :])
        acc = jnp.zeros((BLK, WCOL), jnp.float32)
        for s in range(0, NEAR, 2):
            e0, e1 = near[b, s], near[b, s + 1]
            i0, i1 = jnp.maximum(e0, 0), jnp.maximum(e1, 0)
            sources = jnp.concatenate([grp[i0, 0:BLK, :], grp[i1, 0:BLK, :]], axis=0)
            sn = jnp.concatenate(
                [
                    gn[i0] + jnp.where(e0 >= 0, 0.0, 1e30),
                    gn[i1] + jnp.where(e1 >= 0, 0.0, 1e30),
                ],
                axis=1,
            )
            w = jnp.concatenate([unpack(grp[i0, BLK:BROWS, :]), unpack(grp[i1, BLK:BROWS, :])], axis=0)
            acc = acc + tile(xt, tn, sources, sn, w)
        out[rows, :] = acc
        return c

    half = blk_dev // 2
    lax.fori_loop(0, half, near_block, 0)
    forward(0, 1)
    level_norms(0, shard_of(1))
    lax.fori_loop(half, blk_dev, near_block, 0)
    forward(0, 2)
    level_norms(0, shard_of(2))
    finish(2)

    def far2(p, c):
        facc[p] = far_pair(2, p)
        return c

    def far1(p, c):
        facc[p] = facc[p] + far_pair(1, p)
        return c

    lax.fori_loop(0, n_src * pairs, far2, 0)
    forward(0, 3)
    level_norms(0, shard_of(3))
    finish(1)
    lax.fori_loop(0, n_src * pairs, far1, 0)
    finish(0)

    for j in range(1, n_src):
        def far0(p, c, j=j):
            at = s_peer(j) * pairs + p
            red_out[j, p] = (facc[at] + far_pair(0, at)).astype(jnp.bfloat16)
            return c

        lax.fori_loop(0, pairs, far0, 0)
        r_copy(j).start()

    def far_own(p, c):
        at = src * pairs + p
        facc[at] = facc[at] + far_pair(0, at)
        return c

    lax.fori_loop(0, pairs, far_own, 0)
    for j in range(1, n_src):
        r_copy(j).wait_recv()

    def last(p, c):
        total = facc[src * pairs + p]
        for j in range(1, n_src):
            total = total + red_in[j, p].astype(jnp.float32)
        for h in range(2):
            rows = pl.ds(pl.multiple_of((2 * p + h) * BLK, BLK), BLK)
            out[rows, :] = out[rows, :] + total[:, h * WCOL : (h + 1) * WCOL]
        return c

    lax.fori_loop(0, pairs, last, 0)

    for l in (2, 1, 0):
        for k in range(1, Z):
            z_copy(l, k).wait_send()
        for k in range(Z):
            for j in range(1, X):
                x_copy(l, k, j).wait_send()
    for k in range(1, n_src):
        g_copy(k).wait_send()
        r_copy(k).wait_send()


def shards(n_tgt, n_src, points, weights, near_list, far_list, skel_index, equiv_weights):
    point_dev = points.shape[0]
    blk_dev = point_dev // BLK
    level_nodes = [blk_dev // (4 * 2**l) for l in range(LEVELS)]
    group = n_src * blk_dev
    X = n_tgt // Z
    vmem, smem = pl.BlockSpec(memory_space=pltpu.VMEM), pl.BlockSpec(memory_space=pltpu.SMEM)
    bf16, f32 = jnp.bfloat16, jnp.float32
    dma = pltpu.SemaphoreType.DMA
    return pl.pallas_call(
        functools.partial(kernel, n_tgt, n_src, blk_dev, level_nodes),
        out_shape=jax.ShapeDtypeStruct((point_dev, WCOL), f32),
        in_specs=[vmem, vmem, vmem, vmem, smem, smem],
        out_specs=vmem,
        scratch_shapes=[
            pltpu.VMEM((group, BROWS, E), bf16),
            pltpu.VMEM((group, 1, BLK), f32),
            *[pltpu.VMEM((n_tgt * n, NROWS, E), bf16) for n in level_nodes],
            *[pltpu.VMEM((n_tgt * n, 1, RANK), f32) for n in level_nodes],
            pltpu.VMEM((group // 2, BLK, 2 * WCOL), f32),
            pltpu.VMEM((n_src, blk_dev // 2, BLK, 2 * WCOL), bf16),
            pltpu.VMEM((n_src, blk_dev // 2, BLK, 2 * WCOL), bf16),
            dma((n_src,)), dma((n_src,)),
            dma((LEVELS * Z,)), dma((LEVELS * Z,)),
            dma((LEVELS * Z * X,)), dma((LEVELS * Z * X,)),
            dma((n_src,)), dma((n_src,)),
        ],
        compiler_params=pltpu.CompilerParams(
            collective_id=0, has_side_effects=True, vmem_limit_bytes=56 * 2**20
        ),
    )(
        points, weights, skel_index.T, equiv_weights, near_list, far_list[:, :, 0].T,
    )


def solution(mesh):
    in_specs = (
        P(("tgt", "src"), None),
        P(("tgt", "src"), None),
        P(("tgt", "src"), None),
        P("tgt", None, "src"),
        P(("tgt", "src"), None),
        P(("tgt", "src"), None, None),
    )
    out_specs = P(("tgt", "src"), None)
    body = functools.partial(shards, mesh.shape["tgt"], mesh.shape["src"])
    return jax.shard_map(body, mesh=mesh, in_specs=in_specs, out_specs=out_specs, check_vma=False)
```

```python
import functools

import jax
import jax.numpy as jnp
from jax import lax
from jax.experimental import pallas as pl
from jax.experimental.pallas import tpu as pltpu
from jax.sharding import PartitionSpec as P

E = 256
WCOL = 64
BLK = 128
RANK = 256
NEAR = 16
LEVELS = 3
Z = 4

BROWS = BLK + BLK // 4
NROWS = RANK + RANK // 4
MESH = pl.DeviceIdType.MESH


def pack(w):
    q = w.shape[0] // 4
    return jnp.concatenate([w[k * q : (k + 1) * q, :] for k in range(4)], axis=1)


def unpack(p):
    return jnp.concatenate([p[:, k * WCOL : (k + 1) * WCOL] for k in range(4)], axis=0)


def row_norms(x):
    sq = jnp.square(x.astype(jnp.float32))
    hi = sq.astype(jnp.bfloat16)
    lo = (sq - hi.astype(jnp.float32)).astype(jnp.bfloat16)
    twos = jnp.full((16, E), 2.0, jnp.bfloat16)
    dims = (((1,), (1,)), ((), ()))
    total = lax.dot_general(twos, hi, dims, preferred_element_type=jnp.float32)
    total = total + lax.dot_general(twos, lo, dims, preferred_element_type=jnp.float32)
    return total[0:1, :]


def targets_of(x):
    sq = jnp.square(x.astype(jnp.float32))
    return x * jnp.bfloat16(4.0), 2.0 * jnp.sum(sq, axis=1, keepdims=True)


def tile(xt, tn, src, sn, w):
    d = lax.dot_general(xt, src, (((1,), (1,)), ((), ())), preferred_element_type=jnp.float32)
    k = jnp.exp((d - tn) - sn).astype(jnp.bfloat16)
    return jnp.dot(k, w, preferred_element_type=jnp.float32)


def kernel(
    n_tgt, n_src, blk_dev, level_nodes,
    pts, wts, skel, ew, near, far, out,
    grp, gn, l0, l1, l2, n0, n1, n2, facc, red_out, red_in,
    gs, gr, zs, zr, xs, xr, rs, rr,
):
    X = n_tgt // Z
    Y = n_src // 2
    tgt, src = lax.axis_index("tgt"), lax.axis_index("src")
    z, x = tgt // X, tgt % X
    y, core = src // 2, src % 2
    levels, norms = (l0, l1, l2), (n0, n1, n2)
    pairs = blk_dev // 2
    half0 = level_nodes[0] // 2
    items = ((2, 0, level_nodes[2]), (1, 0, level_nodes[1]), (0, 0, half0), (0, half0, half0))
    mates = [(dy, dc) for dy in range(1, Y) for dc in range(2)] + [(0, 1)]

    def x_peer(j):
        return z * X + lax.rem(x + j, X)

    def x_from(j):
        return lax.rem(x - j + X, X)

    def s_peer(dy, dc):
        return lax.rem(y + dy, Y) * 2 + (1 - core if dc else core)

    barrier = pltpu.get_barrier_semaphore()

    def greet(t, s):
        pl.semaphore_signal(barrier, inc=1, device_id=(t, s), device_id_type=MESH)

    @pl.when(z > 0)
    def _():
        greet(tgt - X, src)

    @pl.when(z < Z - 1)
    def _():
        greet(tgt + X, src)

    for j in range(1, X):
        greet(x_peer(j), src)
    for dy, dc in mates:
        greet(tgt, s_peer(dy, dc))

    def nodes(i, owner):
        l, first, count = items[i]
        return levels[l].at[pl.ds(owner * level_nodes[l] + first, count)]

    def z_copy(i, d, k, col, j):
        held = nodes(i, (z - d * k) * X + col)
        at = ((i * 2 + (d + 1) // 2) * Z + k) * X + j
        return pltpu.make_async_remote_copy(
            held, held, zs.at[at], zr.at[at], (tgt + d * X, src), MESH
        )

    def x_copy(i, d, k, j):
        held = nodes(i, (z - d * k) * X + x)
        at = ((i * 2 + (d + 1) // 2) * Z + k) * X + j
        return pltpu.make_async_remote_copy(held, held, xs.at[at], xr.at[at], (x_peer(j), src), MESH)

    def has(d, k):
        return (z >= k) if d > 0 else (z + k <= Z - 1)

    def more(d):
        return (z < Z - 1) if d > 0 else (z > 0)

    def g_copy(k):
        own = grp.at[pl.ds(src * blk_dev, blk_dev)]
        return pltpu.make_async_remote_copy(own, own, gs.at[k], gr.at[k], (tgt, s_peer(k, 0)), MESH)

    def c_copy(k):
        row = (lax.rem(y - k + Y, Y) * 2 + core) * blk_dev
        held = grp.at[pl.ds(row, blk_dev)]
        return pltpu.make_async_remote_copy(
            held, held, gs.at[Y + k], gr.at[Y + k], (tgt, s_peer(0, 1)), MESH
        )

    def r_copy(m):
        return pltpu.make_async_remote_copy(
            red_out.at[m], red_in.at[m], rs.at[m], rr.at[m], (tgt, s_peer(*mates[m])), MESH
        )

    def gather_level(l):
        size = 4 * BLK * 2**l
        start = sum(level_nodes[:l])
        for r in range(level_nodes[l]):
            node = start + r
            acc = jnp.zeros((RANK, E), jnp.float32)
            for c in range(size // 512):
                base = r * size + c * 512
                pick = lax.broadcasted_iota(jnp.int32, (RANK, 512), 1) == skel[:, node : node + 1] - base
                pick = jnp.where(pick, 1.0, 0.0).astype(jnp.bfloat16)
                acc = acc + jnp.dot(pick, pts[base : base + 512, :], preferred_element_type=jnp.float32)
            at = tgt * level_nodes[l] + r
            levels[l][at, 0:RANK, :] = acc.astype(jnp.bfloat16)
            levels[l][at, RANK:NROWS, :] = pack(ew[node])

    def item_norms(i, owner):
        l, first, count = items[i]
        for r in range(count):
            at = owner * level_nodes[l] + first + r
            norms[l][at] = row_norms(levels[l][at, 0:RANK, :])

    def send_own(i):
        for d in (1, -1):
            @pl.when(more(d))
            def _(d=d):
                z_copy(i, d, 0, x, 0).start()
        for j in range(1, X):
            x_copy(i, 1, 0, j).start()

    def forward(i, d, k, norm=True):
        @pl.when(has(d, k))
        def _():
            z_copy(i, d, k - 1, x, 0).wait_recv()
            if k < Z - 1:
                @pl.when(more(d))
                def _():
                    z_copy(i, d, k, x, 0).start()
            if i > 0:
                for j in range(1, X):
                    x_copy(i, d, k, j).start()
            if norm:
                item_norms(i, (z - d * k) * X + x)

    def forward_other(d, k):
        @pl.when(has(d, k))
        def _():
            for j in range(1, X):
                z_copy(0, d, k - 1, x_from(j), j).wait_recv()
                if k < Z - 1:
                    @pl.when(more(d))
                    def _(j=j):
                        z_copy(0, d, k, x_from(j), j).start()
                item_norms(0, (z - d * k) * X + x_from(j))

    def crossed(i, d, k):
        @pl.when(has(d, k))
        def _():
            for j in range(1, X):
                x_copy(i, d, k, j).wait_recv()
                item_norms(i, (z - d * k) * X + x_from(j))

    gather_level(2)
    pl.semaphore_wait(
        barrier, (z > 0).astype(jnp.int32) + (z < Z - 1).astype(jnp.int32) + (X - 1) + len(mates)
    )
    send_own(0)
    gather_level(1)
    send_own(1)
    for j in range(1, X):
        x_copy(0, 1, 0, j).wait_recv()
        for d in (1, -1):
            @pl.when(more(d))
            def _(d=d, j=j):
                z_copy(0, d, 0, x_from(j), j).start()
    gather_level(0)
    send_own(2)

    def pack_block(b, c):
        at = src * blk_dev + b
        grp[at, 0:BLK, :] = pts[pl.ds(pl.multiple_of(b * BLK, BLK), BLK), :]
        grp[at, BLK:BROWS, :] = pack(wts[pl.ds(pl.multiple_of(b * BLK, BLK), BLK), :])
        return c

    lax.fori_loop(0, blk_dev, pack_block, 0)
    for k in range(1, Y):
        g_copy(k).start()
    c_copy(0).start()
    for i in range(4):
        item_norms(i, tgt)
    for j in range(1, X):
        item_norms(0, z * X + x_from(j))

    ways = [(d, k) for k in range(1, Z) for d in (1, -1)]
    for k in range(1, Z):
        for d in (1, -1):
            forward(0, d, k)
            forward(1, d, k)
        for d in (1, -1):
            forward_other(d, k)
        if k == 1:
            send_own(3)
            for j in range(1, Y):
                g_copy(j).wait_recv()
                c_copy(j).start()

    for k in range(Y):
        c_copy(k).wait_recv()

    def group_norms(b, c):
        gn[b] = row_norms(grp[b, 0:BLK, :])
        return c

    lax.fori_loop(0, n_src * blk_dev, group_norms, 0, unroll=4)

    def far_block(l, b):
        xt, tn = targets_of(grp[b, 0:BLK, :])
        e = far[l, b]
        i = jnp.maximum(e, 0)
        sn = norms[l][i] + jnp.where(e >= 0, 0.0, 1e30)
        return tile(xt, tn, levels[l][i, 0:RANK, :], sn, unpack(levels[l][i, RANK:NROWS, :]))

    def far_pair(l, p):
        return jnp.concatenate([far_block(l, 2 * p), far_block(l, 2 * p + 1)], axis=1)

    def near_block(b, c):
        rows = pl.ds(pl.multiple_of(b * BLK, BLK), BLK)
        xt, tn = targets_of(pts[rows, :])
        acc = jnp.zeros((BLK, WCOL), jnp.float32)
        for s in range(0, NEAR, 2):
            e0, e1 = near[b, s], near[b, s + 1]
            i0, i1 = jnp.maximum(e0, 0), jnp.maximum(e1, 0)
            sources = jnp.concatenate([grp[i0, 0:BLK, :], grp[i1, 0:BLK, :]], axis=0)
            sn = jnp.concatenate(
                [
                    gn[i0] + jnp.where(e0 >= 0, 0.0, 1e30),
                    gn[i1] + jnp.where(e1 >= 0, 0.0, 1e30),
                ],
                axis=1,
            )
            w = jnp.concatenate([unpack(grp[i0, BLK:BROWS, :]), unpack(grp[i1, BLK:BROWS, :])], axis=0)
            acc = acc + tile(xt, tn, sources, sn, w)
        out[rows, :] = acc
        return c

    def far2(p, c):
        facc[p] = far_pair(2, p)
        return c

    def far1(p, c):
        facc[p] = facc[p] + far_pair(1, p)
        return c

    count = n_src * pairs
    forward(2, 1, 1)
    forward(2, -1, 1)
    lax.fori_loop(0, blk_dev // 4, near_block, 0)
    forward(3, 1, 1)
    forward(3, -1, 1)
    lax.fori_loop(blk_dev // 4, blk_dev // 2, near_block, 0)
    forward(2, 1, 2)
    forward(2, -1, 2)
    lax.fori_loop(blk_dev // 2, blk_dev * 3 // 4, near_block, 0)
    forward(3, 1, 2)
    forward(3, -1, 2)
    lax.fori_loop(blk_dev * 3 // 4, blk_dev, near_block, 0)
    forward(2, 1, 3)
    forward(2, -1, 3)
    lax.fori_loop(0, count // 2, far2, 0, unroll=2)
    forward(3, 1, 3)
    forward(3, -1, 3)
    lax.fori_loop(count // 2, count, far2, 0, unroll=2)
    crossed(1, 1, 0)
    for d, k in ways:
        crossed(1, d, k)
    lax.fori_loop(0, count, far1, 0, unroll=2)
    for i in (2, 3):
        crossed(i, 1, 0)
    for d, k in ways:
        for i in (2, 3):
            crossed(i, d, k)

    for m, mate in enumerate(mates):
        def far0(p, c, m=m, mate=mate):
            at = s_peer(*mate) * pairs + p
            red_out[m, p] = (facc[at] + far_pair(0, at)).astype(jnp.bfloat16)
            return c

        lax.fori_loop(0, pairs, far0, 0, unroll=2)
        r_copy(m).start()

    def far_own(p, c):
        at = src * pairs + p
        facc[at] = facc[at] + far_pair(0, at)
        return c

    lax.fori_loop(0, pairs, far_own, 0, unroll=2)
    for m in range(len(mates)):
        r_copy(m).wait_recv()

    def last(p, c):
        total = facc[src * pairs + p]
        for m in range(len(mates)):
            total = total + red_in[m, p].astype(jnp.float32)
        for h in range(2):
            rows = pl.ds(pl.multiple_of((2 * p + h) * BLK, BLK), BLK)
            out[rows, :] = out[rows, :] + total[:, h * WCOL : (h + 1) * WCOL]
        return c

    lax.fori_loop(0, pairs, last, 0)

    for i in range(4):
        for j in range(1, X):
            x_copy(i, 1, 0, j).wait_send()
        for d, k in [(1, 0), (-1, 0)] + ways:
            if k < Z - 1:
                @pl.when(has(d, k) & more(d))
                def _(i=i, d=d, k=k):
                    z_copy(i, d, k, x, 0).wait_send()
                    if i == 0:
                        for j in range(1, X):
                            z_copy(0, d, k, x_from(j), j).wait_send()
            if k > 0 and i > 0:
                @pl.when(has(d, k))
                def _(i=i, d=d, k=k):
                    for j in range(1, X):
                        x_copy(i, d, k, j).wait_send()
    for k in range(1, Y):
        g_copy(k).wait_send()
    for k in range(Y):
        c_copy(k).wait_send()
    for m in range(len(mates)):
        r_copy(m).wait_send()


def shards(n_tgt, n_src, points, weights, near_list, far_list, skel_index, equiv_weights):
    point_dev = points.shape[0]
    blk_dev = point_dev // BLK
    level_nodes = [blk_dev // (4 * 2**l) for l in range(LEVELS)]
    group = n_src * blk_dev
    X = n_tgt // Z
    vmem, smem = pl.BlockSpec(memory_space=pltpu.VMEM), pl.BlockSpec(memory_space=pltpu.SMEM)
    bf16, f32 = jnp.bfloat16, jnp.float32
    dma = pltpu.SemaphoreType.DMA
    return pl.pallas_call(
        functools.partial(kernel, n_tgt, n_src, blk_dev, level_nodes),
        out_shape=jax.ShapeDtypeStruct((point_dev, WCOL), f32),
        in_specs=[vmem, vmem, vmem, vmem, smem, smem],
        out_specs=vmem,
        scratch_shapes=[
            pltpu.VMEM((group, BROWS, E), bf16),
            pltpu.VMEM((group, 1, BLK), f32),
            *[pltpu.VMEM((n_tgt * n, NROWS, E), bf16) for n in level_nodes],
            *[pltpu.VMEM((n_tgt * n, 1, RANK), f32) for n in level_nodes],
            pltpu.VMEM((group // 2, BLK, 2 * WCOL), f32),
            pltpu.VMEM((n_src, blk_dev // 2, BLK, 2 * WCOL), bf16),
            pltpu.VMEM((n_src, blk_dev // 2, BLK, 2 * WCOL), bf16),
            dma((n_src,)), dma((n_src,)),
            dma((8 * Z * X,)), dma((8 * Z * X,)),
            dma((8 * Z * X,)), dma((8 * Z * X,)),
            dma((n_src,)), dma((n_src,)),
        ],
        compiler_params=pltpu.CompilerParams(
            collective_id=0, has_side_effects=True, vmem_limit_bytes=56 * 2**20
        ),
    )(
        points, weights, skel_index.T, equiv_weights, near_list, far_list[:, :, 0].T,
    )


def solution(mesh):
    in_specs = (
        P(("tgt", "src"), None),
        P(("tgt", "src"), None),
        P(("tgt", "src"), None),
        P("tgt", None, "src"),
        P(("tgt", "src"), None),
        P(("tgt", "src"), None, None),
    )
    out_specs = P(("tgt", "src"), None)
    body = functools.partial(shards, mesh.shape["tgt"], mesh.shape["src"])
    return jax.shard_map(body, mesh=mesh, in_specs=in_specs, out_specs=out_specs, check_vma=False)
```

```python
import functools

import jax
import jax.numpy as jnp
from jax import lax
from jax.experimental import pallas as pl
from jax.experimental.pallas import tpu as pltpu
from jax.sharding import PartitionSpec as P

E = 256
WCOL = 64
BLK = 128
RANK = 256
NEAR = 16
LEVELS = 3
Z = 4

BROWS = BLK + BLK // 4
NROWS = RANK + RANK // 4
MESH = pl.DeviceIdType.MESH


def pack(w):
    q = w.shape[0] // 4
    return jnp.concatenate([w[k * q : (k + 1) * q, :] for k in range(4)], axis=1)


def unpack(p):
    return jnp.concatenate([p[:, k * WCOL : (k + 1) * WCOL] for k in range(4)], axis=0)


def row_norms(x):
    sq = jnp.square(x.astype(jnp.float32))
    hi = sq.astype(jnp.bfloat16)
    lo = (sq - hi.astype(jnp.float32)).astype(jnp.bfloat16)
    twos = jnp.full((16, E), 2.0, jnp.bfloat16)
    dims = (((1,), (1,)), ((), ()))
    total = lax.dot_general(twos, hi, dims, preferred_element_type=jnp.float32)
    total = total + lax.dot_general(twos, lo, dims, preferred_element_type=jnp.float32)
    return total[0:1, :]


def targets_of(x):
    sq = jnp.square(x.astype(jnp.float32))
    return x * jnp.bfloat16(4.0), 2.0 * jnp.sum(sq, axis=1, keepdims=True)


def tile(xt, tn, src, sn, w):
    d = lax.dot_general(xt, src, (((1,), (1,)), ((), ())), preferred_element_type=jnp.float32)
    k = jnp.exp((d - tn) - sn).astype(jnp.bfloat16)
    return jnp.dot(k, w, preferred_element_type=jnp.float32)


def kernel(
    n_tgt, n_src, blk_dev, level_nodes,
    pts, wts, skel, ew, near, far, out,
    grp, gn, l0, l1, l2, n0, n1, n2, facc, red_out, red_in,
    gs, gr, zs, zr, xs, xr, rs, rr,
):
    X = n_tgt // Z
    Y = n_src // 2
    tgt, src = lax.axis_index("tgt"), lax.axis_index("src")
    z, x = tgt // X, tgt % X
    y, core = src // 2, src % 2
    levels, norms = (l0, l1, l2), (n0, n1, n2)
    pairs = blk_dev // 2
    part0 = level_nodes[0] // 4
    items = ((2, 0, level_nodes[2]), (1, 0, level_nodes[1]), *((0, q * part0, part0) for q in range(4)))
    mates = [(dy, dc) for dy in range(1, Y) for dc in range(2)] + [(0, 1)]

    def x_peer(j):
        return z * X + lax.rem(x + j, X)

    def x_from(j):
        return lax.rem(x - j + X, X)

    def s_peer(dy, dc):
        return lax.rem(y + dy, Y) * 2 + (1 - core if dc else core)

    barrier = pltpu.get_barrier_semaphore()

    def greet(t, s):
        pl.semaphore_signal(barrier, inc=1, device_id=(t, s), device_id_type=MESH)

    @pl.when(z > 0)
    def _():
        greet(tgt - X, src)

    @pl.when(z < Z - 1)
    def _():
        greet(tgt + X, src)

    for j in range(1, X):
        greet(x_peer(j), src)
    for dy, dc in mates:
        greet(tgt, s_peer(dy, dc))

    def nodes(i, owner):
        l, first, count = items[i]
        return levels[l].at[pl.ds(owner * level_nodes[l] + first, count)]

    def z_copy(i, d, k, col, j):
        held = nodes(i, (z - d * k) * X + col)
        at = ((i * 2 + (d + 1) // 2) * Z + k) * X + j
        return pltpu.make_async_remote_copy(
            held, held, zs.at[at], zr.at[at], (tgt + d * X, src), MESH
        )

    def x_copy(i, d, k, j):
        held = nodes(i, (z - d * k) * X + x)
        at = ((i * 2 + (d + 1) // 2) * Z + k) * X + j
        return pltpu.make_async_remote_copy(held, held, xs.at[at], xr.at[at], (x_peer(j), src), MESH)

    def has(d, k):
        return (z >= k) if d > 0 else (z + k <= Z - 1)

    def more(d):
        return (z < Z - 1) if d > 0 else (z > 0)

    def g_copy(k):
        own = grp.at[pl.ds(src * blk_dev, blk_dev)]
        return pltpu.make_async_remote_copy(own, own, gs.at[k], gr.at[k], (tgt, s_peer(k, 0)), MESH)

    def c_copy(k):
        row = (lax.rem(y - k + Y, Y) * 2 + core) * blk_dev
        held = grp.at[pl.ds(row, blk_dev)]
        return pltpu.make_async_remote_copy(
            held, held, gs.at[Y + k], gr.at[Y + k], (tgt, s_peer(0, 1)), MESH
        )

    def r_copy(m):
        return pltpu.make_async_remote_copy(
            red_out.at[m], red_in.at[m], rs.at[m], rr.at[m], (tgt, s_peer(*mates[m])), MESH
        )

    def gather_level(l):
        size = 4 * BLK * 2**l
        start = sum(level_nodes[:l])
        for r in range(level_nodes[l]):
            node = start + r
            acc = jnp.zeros((RANK, E), jnp.float32)
            for c in range(size // 512):
                base = r * size + c * 512
                pick = lax.broadcasted_iota(jnp.int32, (RANK, 512), 1) == skel[:, node : node + 1] - base
                pick = jnp.where(pick, 1.0, 0.0).astype(jnp.bfloat16)
                acc = acc + jnp.dot(pick, pts[base : base + 512, :], preferred_element_type=jnp.float32)
            at = tgt * level_nodes[l] + r
            levels[l][at, 0:RANK, :] = acc.astype(jnp.bfloat16)
            levels[l][at, RANK:NROWS, :] = pack(ew[node])

    def item_norms(i, owner):
        l, first, count = items[i]
        for r in range(count):
            at = owner * level_nodes[l] + first + r
            norms[l][at] = row_norms(levels[l][at, 0:RANK, :])

    def send_own(i):
        for d in (1, -1):
            @pl.when(more(d))
            def _(d=d):
                z_copy(i, d, 0, x, 0).start()
        for j in range(1, X):
            x_copy(i, 1, 0, j).start()

    def forward(i, d, k, norm=True):
        @pl.when(has(d, k))
        def _():
            z_copy(i, d, k - 1, x, 0).wait_recv()
            if k < Z - 1:
                @pl.when(more(d))
                def _():
                    z_copy(i, d, k, x, 0).start()
            if i > 0:
                for j in range(1, X):
                    x_copy(i, d, k, j).start()
            if norm:
                item_norms(i, (z - d * k) * X + x)

    def forward_other(d, k):
        @pl.when(has(d, k))
        def _():
            for j in range(1, X):
                z_copy(0, d, k - 1, x_from(j), j).wait_recv()
                if k < Z - 1:
                    @pl.when(more(d))
                    def _(j=j):
                        z_copy(0, d, k, x_from(j), j).start()
                item_norms(0, (z - d * k) * X + x_from(j))

    def crossed(i, d, k):
        @pl.when(has(d, k))
        def _():
            for j in range(1, X):
                x_copy(i, d, k, j).wait_recv()
                item_norms(i, (z - d * k) * X + x_from(j))

    gather_level(2)
    pl.semaphore_wait(
        barrier, (z > 0).astype(jnp.int32) + (z < Z - 1).astype(jnp.int32) + (X - 1) + len(mates)
    )
    send_own(0)
    gather_level(1)
    send_own(1)
    for j in range(1, X):
        x_copy(0, 1, 0, j).wait_recv()
        for d in (1, -1):
            @pl.when(more(d))
            def _(d=d, j=j):
                z_copy(0, d, 0, x_from(j), j).start()
    gather_level(0)
    for i in range(2, len(items)):
        send_own(i)

    def pack_block(b, c):
        at = src * blk_dev + b
        grp[at, 0:BLK, :] = pts[pl.ds(pl.multiple_of(b * BLK, BLK), BLK), :]
        grp[at, BLK:BROWS, :] = pack(wts[pl.ds(pl.multiple_of(b * BLK, BLK), BLK), :])
        return c

    lax.fori_loop(0, blk_dev, pack_block, 0)
    for k in range(1, Y):
        g_copy(k).start()
    c_copy(0).start()
    for i in range(len(items)):
        item_norms(i, tgt)
    for j in range(1, X):
        item_norms(0, z * X + x_from(j))

    ways = [(d, k) for k in range(1, Z) for d in (1, -1)]
    for k in range(1, Z):
        for d in (1, -1):
            forward(0, d, k)
            forward(1, d, k)
        for d in (1, -1):
            forward_other(d, k)
        if k == 1:
            for j in range(1, Y):
                g_copy(j).wait_recv()
                c_copy(j).start()

    for k in range(Y):
        c_copy(k).wait_recv()

    def group_norms(b, c):
        gn[b] = row_norms(grp[b, 0:BLK, :])
        return c

    lax.fori_loop(0, n_src * blk_dev, group_norms, 0, unroll=4)

    def far_block(l, b):
        xt, tn = targets_of(grp[b, 0:BLK, :])
        e = far[l, b]
        i = jnp.maximum(e, 0)
        sn = norms[l][i] + jnp.where(e >= 0, 0.0, 1e30)
        return tile(xt, tn, levels[l][i, 0:RANK, :], sn, unpack(levels[l][i, RANK:NROWS, :]))

    def far_pair(l, p):
        return jnp.concatenate([far_block(l, 2 * p), far_block(l, 2 * p + 1)], axis=1)

    def near_block(b, c):
        rows = pl.ds(pl.multiple_of(b * BLK, BLK), BLK)
        xt, tn = targets_of(pts[rows, :])
        acc = jnp.zeros((BLK, WCOL), jnp.float32)
        for s in range(0, NEAR, 2):
            e0, e1 = near[b, s], near[b, s + 1]
            i0, i1 = jnp.maximum(e0, 0), jnp.maximum(e1, 0)
            sources = jnp.concatenate([grp[i0, 0:BLK, :], grp[i1, 0:BLK, :]], axis=0)
            sn = jnp.concatenate(
                [
                    gn[i0] + jnp.where(e0 >= 0, 0.0, 1e30),
                    gn[i1] + jnp.where(e1 >= 0, 0.0, 1e30),
                ],
                axis=1,
            )
            w = jnp.concatenate([unpack(grp[i0, BLK:BROWS, :]), unpack(grp[i1, BLK:BROWS, :])], axis=0)
            acc = acc + tile(xt, tn, sources, sn, w)
        out[rows, :] = acc
        return c

    def far2(p, c):
        facc[p] = far_pair(2, p)
        return c

    def far1(p, c):
        facc[p] = facc[p] + far_pair(1, p)
        return c

    count = n_src * pairs
    for i in (2, 3):
        forward(i, 1, 1)
        forward(i, -1, 1)
    lax.fori_loop(0, blk_dev // 4, near_block, 0)
    for i in (4, 5):
        forward(i, 1, 1)
        forward(i, -1, 1)
    lax.fori_loop(blk_dev // 4, blk_dev // 2, near_block, 0)
    for i in (2, 3):
        forward(i, 1, 2)
        forward(i, -1, 2)
    lax.fori_loop(blk_dev // 2, blk_dev * 3 // 4, near_block, 0)
    for i in (4, 5):
        forward(i, 1, 2)
        forward(i, -1, 2)
    lax.fori_loop(blk_dev * 3 // 4, blk_dev, near_block, 0)
    for i in (2, 3):
        forward(i, 1, 3)
        forward(i, -1, 3)
    lax.fori_loop(0, count // 2, far2, 0, unroll=2)
    for i in (4, 5):
        forward(i, 1, 3)
        forward(i, -1, 3)
    lax.fori_loop(count // 2, count, far2, 0, unroll=2)
    crossed(1, 1, 0)
    for d, k in ways:
        crossed(1, d, k)
    lax.fori_loop(0, count, far1, 0, unroll=2)
    for i in range(2, 6):
        crossed(i, 1, 0)
    for d, k in ways:
        for i in range(2, 6):
            crossed(i, d, k)

    for m, mate in enumerate(mates):
        def far0(p, c, m=m, mate=mate):
            at = s_peer(*mate) * pairs + p
            red_out[m, p] = (facc[at] + far_pair(0, at)).astype(jnp.bfloat16)
            return c

        lax.fori_loop(0, pairs, far0, 0, unroll=4)
        r_copy(m).start()

    def far_own(p, c):
        at = src * pairs + p
        facc[at] = facc[at] + far_pair(0, at)
        return c

    lax.fori_loop(0, pairs, far_own, 0, unroll=4)
    for m in range(len(mates)):
        r_copy(m).wait_recv()

    def last(p, c):
        total = facc[src * pairs + p]
        for m in range(len(mates)):
            total = total + red_in[m, p].astype(jnp.float32)
        for h in range(2):
            rows = pl.ds(pl.multiple_of((2 * p + h) * BLK, BLK), BLK)
            out[rows, :] = out[rows, :] + total[:, h * WCOL : (h + 1) * WCOL]
        return c

    lax.fori_loop(0, pairs, last, 0)

    for i in range(len(items)):
        for j in range(1, X):
            x_copy(i, 1, 0, j).wait_send()
        for d, k in [(1, 0), (-1, 0)] + ways:
            if k < Z - 1:
                @pl.when(has(d, k) & more(d))
                def _(i=i, d=d, k=k):
                    z_copy(i, d, k, x, 0).wait_send()
                    if i == 0:
                        for j in range(1, X):
                            z_copy(0, d, k, x_from(j), j).wait_send()
            if k > 0 and i > 0:
                @pl.when(has(d, k))
                def _(i=i, d=d, k=k):
                    for j in range(1, X):
                        x_copy(i, d, k, j).wait_send()
    for k in range(1, Y):
        g_copy(k).wait_send()
    for k in range(Y):
        c_copy(k).wait_send()
    for m in range(len(mates)):
        r_copy(m).wait_send()


def shards(n_tgt, n_src, points, weights, near_list, far_list, skel_index, equiv_weights):
    point_dev = points.shape[0]
    blk_dev = point_dev // BLK
    level_nodes = [blk_dev // (4 * 2**l) for l in range(LEVELS)]
    group = n_src * blk_dev
    X = n_tgt // Z
    vmem, smem = pl.BlockSpec(memory_space=pltpu.VMEM), pl.BlockSpec(memory_space=pltpu.SMEM)
    bf16, f32 = jnp.bfloat16, jnp.float32
    dma = pltpu.SemaphoreType.DMA
    return pl.pallas_call(
        functools.partial(kernel, n_tgt, n_src, blk_dev, level_nodes),
        out_shape=jax.ShapeDtypeStruct((point_dev, WCOL), f32),
        in_specs=[vmem, vmem, vmem, vmem, smem, smem],
        out_specs=vmem,
        scratch_shapes=[
            pltpu.VMEM((group, BROWS, E), bf16),
            pltpu.VMEM((group, 1, BLK), f32),
            *[pltpu.VMEM((n_tgt * n, NROWS, E), bf16) for n in level_nodes],
            *[pltpu.VMEM((n_tgt * n, 1, RANK), f32) for n in level_nodes],
            pltpu.VMEM((group // 2, BLK, 2 * WCOL), f32),
            pltpu.VMEM((n_src, blk_dev // 2, BLK, 2 * WCOL), bf16),
            pltpu.VMEM((n_src, blk_dev // 2, BLK, 2 * WCOL), bf16),
            dma((n_src,)), dma((n_src,)),
            dma((12 * Z * X,)), dma((12 * Z * X,)),
            dma((12 * Z * X,)), dma((12 * Z * X,)),
            dma((n_src,)), dma((n_src,)),
        ],
        compiler_params=pltpu.CompilerParams(
            collective_id=0, has_side_effects=True, vmem_limit_bytes=56 * 2**20
        ),
    )(
        points, weights, skel_index.T, equiv_weights, near_list, far_list[:, :, 0].T,
    )


def solution(mesh):
    in_specs = (
        P(("tgt", "src"), None),
        P(("tgt", "src"), None),
        P(("tgt", "src"), None),
        P("tgt", None, "src"),
        P(("tgt", "src"), None),
        P(("tgt", "src"), None, None),
    )
    out_specs = P(("tgt", "src"), None)
    body = functools.partial(shards, mesh.shape["tgt"], mesh.shape["src"])
    return jax.shard_map(body, mesh=mesh, in_specs=in_specs, out_specs=out_specs, check_vma=False)
```
